32 devices in a mesh: req: 4 (over z), vocab: 8 (over y, x, core).
Axes of the slice: x: 2, y: 2, z: 4, core: 2. Of those that a mesh axis runs over, the one named last changes fastest.
Arguments:
- hidden_states: bfloat16 [6144, 2048], P(('req', 'vocab')), may hold values from -400 to 400
- norm_gain: float32 [2048], replicated, may hold values from 0.25 to 1.75
- head_weight: bfloat16 [2048, 32000], P(None, 'vocab'), may hold values from -2 to 2
- targets: int32 [6144], P(('req', 'vocab')), may hold values from 0 to 31999
- lengths: int32 [256], P(('req', 'vocab')), may hold values from 1 to 24, as said below
- slot_of: int32 [256], P(('req', 'vocab')), may hold values from 0 to 255, each once
Outputs:
- logprob: float32 [256, 24], P(('req', 'vocab'))
- entropy: float32 [256, 24], P(('req', 'vocab'))
The draws below stay inside these ranges and needn't reach their ends.
Inputs may be any that keep to these rules, and one draw needn't show every extreme that they name: The lengths of the 8 requests of one device sum to at most 128; some device's sum to exactly 128.
All inputs are finite; a program needn't handle non-finite values.
Results may differ from the reference program's by a relative error of at most 0.00097.
Values may be sent and summed in bfloat16 or wider, within the bound.
No kernel may reach another device: no remote copies, remote signals or barrier semaphores. Data moves between devices by JAX's collectives and lax.ppermute only.
A program may use at most 128 MiB of HBM per device.

```python
import math
import jax
import jax.numpy as jnp
import numpy as np
from jax import lax

D = 2048
V = 32000
SEQ_DEV = 8
SEQ_LEN = 24
LIVE_CAP = 128
SEQS = 256
ROWS = 6144


def draw_hidden_states(key, part):
    subkeys = jax.random.split(jax.random.fold_in(key, 11), 3)
    rows_total = SEQS * SEQ_LEN
    random_part = jnp.clip(jax.random.normal(subkeys[0], (rows_total, D), jnp.float32), -4.0, 4.0)
    log_top = jnp.log(10.0)
    row_scale = jnp.exp(jax.random.uniform(subkeys[1], (rows_total, 1), jnp.float32, 0.0, 1.0) * log_top)
    col_scale = jnp.exp(jax.random.uniform(subkeys[2], (1, D), jnp.float32, 0.0, 1.0) * jnp.log(10.0))
    values = random_part * row_scale * col_scale
    return values.astype(jnp.bfloat16)


def draw_head_weight(key, part):
    weight_key = jax.random.fold_in(key, 23)
    weight = jnp.clip(jax.random.normal(weight_key, (D, V), jnp.float32), -4.0, 4.0) * (3.0 / jnp.sqrt(float(D)))
    return weight.astype(jnp.bfloat16)


def draw_lengths(key, part):
    subkeys = jax.random.split(jax.random.fold_in(key, 37), SEQ_DEV + 2)
    owners = SEQS // SEQ_DEV
    budget = jax.random.randint(subkeys[0], (owners,), SEQ_DEV, LIVE_CAP + 1)
    fullest = jax.random.randint(subkeys[1], (), 0, owners)
    owner_ids = jnp.arange(owners, dtype=jnp.int32)
    budget = jnp.where(owner_ids == fullest, LIVE_CAP, budget)
    budget = jnp.where(owner_ids == (fullest + 1) % owners, SEQ_DEV, budget)
    remaining = budget
    pieces = []
    for request in range(SEQ_DEV):
        after = SEQ_DEV - 1 - request
        lowest = jnp.maximum(1, remaining - after * SEQ_LEN)
        highest = jnp.minimum(SEQ_LEN, remaining - after)
        chosen = jax.random.randint(subkeys[request + 2], (owners,), lowest, highest + 1)
        if request == 0:
            chosen = jnp.where(owner_ids == fullest, min(SEQ_LEN, LIVE_CAP), chosen)
        pieces.append(chosen)
        remaining = remaining - chosen
    return jnp.stack(pieces, axis=1).reshape(SEQS).astype(jnp.int32)


def touch_ends(entries, key, least, top_value):
    shape = entries.shape
    index_at = [jax.random.randint(jax.random.fold_in(key, axis), (), 0, shape[axis]) for axis in range(len(shape))]
    entries = entries.at[tuple(index_at)].set(least)
    longest = shape.index(max(shape))
    index_at[longest] = (index_at[longest] + 1) % shape[longest]
    return entries.at[tuple(index_at)].set(top_value)


def rank_table(number_of, slope):
    weights = [(1 << 20) // math.isqrt(grade ** slope) + 1 for grade in range(1, number_of + 1)]
    scale = 1 + sum(weights) // (1 << 30)
    return np.cumsum(np.array([max(1, weight // scale) for weight in weights]))


def ranked_ids(stream_key, shape, count, slope):
    table = rank_table(count, slope)
    lot = jax.random.randint(jax.random.fold_in(stream_key, 1), shape, 0, int(table[count - 1]))
    grade = jnp.searchsorted(jnp.asarray(table, jnp.int32), lot, side="right")
    return jax.random.permutation(jax.random.fold_in(stream_key, 2), count)[grade].astype(jnp.int32)


def setup_inputs(seed: int = 0) -> dict:
    seeds = jax.random.split(jax.random.key(seed), 7)
    return {
        "hidden_states": draw_hidden_states(jax.random.fold_in(seeds[6], 71), 0),
        "norm_gain": jnp.clip(1.0 + 0.15 * jax.random.normal(seeds[1], (D,), jnp.float32), 0.25, 1.75),
        "head_weight": draw_head_weight(jax.random.fold_in(seeds[6], 71), 0),
        "targets": touch_ends(ranked_ids(seeds[3], (ROWS,), V, 2), jax.random.fold_in(seeds[3], 3), 0, V - 1).astype(jnp.int32),
        "lengths": draw_lengths(jax.random.fold_in(seeds[6], 71), 0),
        "slot_of": jax.random.permutation(seeds[5], SEQS).astype(jnp.int32),
    }


eps_norm = 1e-05

def reference(hidden_states, norm_gain, head_weight, targets, lengths, slot_of):
    values = hidden_states.astype(jnp.float32)
    inverse_rms = lax.rsqrt(lax.optimization_barrier(jnp.mean(values * values, axis=1, keepdims=True)) + eps_norm)
    normed = (values * inverse_rms * norm_gain[None, :]).astype(jnp.bfloat16)
    block_count = SEQS // SEQ_DEV
    block_size = SEQ_DEV * SEQ_LEN

    def one_block(block_pair):
        block_rows, block_targets = block_pair
        logits = jnp.dot(block_rows, head_weight, preferred_element_type=jnp.float32)
        row_peak = lax.optimization_barrier(jnp.max(logits, axis=1))
        shifted = logits - row_peak[:, None]
        exponent = jnp.exp(shifted)
        row_total = lax.optimization_barrier(jnp.sum(exponent, axis=1))
        spread = lax.optimization_barrier(jnp.sum(exponent * shifted, axis=1))
        picked = jnp.take_along_axis(logits, block_targets[:, None].astype(jnp.int32), axis=1)[:, 0]
        log_total = jnp.log(row_total)
        return (picked - row_peak - log_total, log_total - spread / row_total)
    slot_logprob, slot_entropy = lax.map(one_block, (normed.reshape(block_count, block_size, D), targets.reshape(block_count, block_size)))
    slot_logprob = slot_logprob.reshape(SEQS, SEQ_LEN)
    slot_entropy = slot_entropy.reshape(SEQS, SEQ_LEN)
    live_mask = jnp.arange(SEQ_LEN, dtype=jnp.int32)[None, :] < lengths[:, None]
    slot_logprob = jnp.where(live_mask, slot_logprob, jnp.zeros_like(slot_logprob))
    slot_entropy = jnp.where(live_mask, slot_entropy, jnp.zeros_like(slot_entropy))
    return (slot_logprob[slot_of], slot_entropy[slot_of])
```

```python
import functools

import jax
import jax.numpy as jnp
from jax import lax
from jax.experimental import pallas as pl
from jax.experimental.pallas import tpu as pltpu
from jax.sharding import PartitionSpec as P

eps_norm = 1e-05
live_cap = 128
extra = 16
tile_vocab = 800
part_vocab = 400
piece_rows = 256
lowest = -1e30
vmem_bytes = 40 * 1024 * 1024
f32 = jnp.float32


def prepare_kernel(lengths_ref, hidden_ref, gain_ref, targets_ref, out_ref):
    rows, depth = hidden_ref.shape
    seq_count = lengths_ref.shape[0]
    seq_len = rows // seq_count
    values = hidden_ref[...].astype(f32)
    inverse_rms = lax.rsqrt(jnp.mean(values * values, axis=1, keepdims=True) + eps_norm)
    normed = (values * inverse_rms * gain_ref[...]).astype(jnp.bfloat16)
    row = lax.broadcasted_iota(jnp.int32, (1, rows), 1)
    sublane = lax.broadcasted_iota(jnp.int32, (extra, live_cap), 0)
    lane = lax.broadcasted_iota(jnp.int32, (extra, live_cap), 1)
    place = jnp.full((1, rows), -1, jnp.int32)
    meta = jnp.zeros((extra, live_cap), jnp.int32)
    start = jnp.int32(0)
    for request in range(seq_count):
        length = lengths_ref[request]
        first = request * seq_len
        place = jnp.where((row >= first) & (row < first + length), row - first + start, place)
        meta = jnp.where(lane == request, start, meta)
        meta = jnp.where(lane == seq_count + request, length, meta)
        start = start + length
    chosen = lax.broadcasted_iota(jnp.int32, (live_cap, rows), 0) == place
    selector = chosen.astype(f32).astype(jnp.bfloat16)
    kept = jnp.dot(selector, normed, preferred_element_type=f32)
    for first in range(0, depth, 128):
        out_ref[first : first + 128, :] = kept[:, first : first + 128].T.astype(jnp.bfloat16)
    target = jnp.sum(jnp.where(chosen, targets_ref[...], 0), axis=1, keepdims=True)
    target = jnp.broadcast_to(target.astype(f32), (live_cap, 128)).T[:extra].astype(jnp.int32)
    meta = jnp.where(sublane == 0, target >> 8, meta)
    meta = jnp.where(sublane == 1, target & 255, meta)
    out_ref[depth:, :] = meta.astype(f32).astype(jnp.bfloat16)


def prepare(hidden_states, norm_gain, targets, lengths):
    rows, depth = hidden_states.shape
    return pl.pallas_call(
        prepare_kernel,
        out_shape=jax.ShapeDtypeStruct((depth + extra, live_cap), jnp.bfloat16),
        in_specs=[
            pl.BlockSpec(memory_space=pltpu.SMEM),
            pl.BlockSpec(memory_space=pltpu.VMEM),
            pl.BlockSpec(memory_space=pltpu.VMEM),
            pl.BlockSpec(memory_space=pltpu.VMEM),
        ],
        out_specs=pl.BlockSpec(memory_space=pltpu.VMEM),
        compiler_params=pltpu.CompilerParams(vmem_limit_bytes=vmem_bytes),
        name="prepare_rows",
    )(lengths, hidden_states, norm_gain.reshape(1, depth), targets.reshape(1, rows))


def stats_kernel(block_count, vocab_cols, steps, *refs):
    blocks = refs[:block_count]
    weight_ref = refs[block_count]
    out_ref, meta_ref = refs[-10:-8]
    rows_ref, logits_ref, peak_ref, total_ref, spread_ref, picked_ref, offset_ref, sems = refs[-8:]
    depth = weight_ref.shape[1]
    rows = block_count * live_cap
    halves = tile_vocab // part_vocab
    units = rows // piece_rows * halves
    step = pl.program_id(0)
    vocab_start = lax.axis_index("vocab") * vocab_cols
    last_valid = vocab_cols - (steps - 1) * tile_vocab

    @pl.when(step == 0)
    def _():
        copies = [
            pltpu.make_async_copy(block, rows_ref.at[:, pl.ds(place * live_cap, live_cap)], sems.at[place])
            for place, block in enumerate(blocks)
        ]
        for copy in copies:
            copy.start()
        peak_ref[...] = jnp.full(peak_ref.shape, lowest, f32)
        total_ref[...] = jnp.zeros(total_ref.shape, f32)
        spread_ref[...] = jnp.zeros(spread_ref.shape, f32)
        picked_ref[...] = jnp.zeros(picked_ref.shape, f32)
        logits_ref[(units - 1) % 2] = jnp.full(logits_ref.shape[1:], lowest, f32)
        for copy in copies:
            copy.wait()
        digits = rows_ref[depth:, :].astype(f32)
        target = (digits[0:1] * 256.0 + digits[1:2]).astype(jnp.int32) - vocab_start
        target = jnp.where((target >= 0) & (target < vocab_cols), target, 2 * steps * tile_vocab)
        offset_ref[...] = target - lax.broadcasted_iota(jnp.int32, (8, rows), 0)
        meta_ref[...] = digits[2:3]

    def absorb(unit, tile):
        slot = unit % 2
        piece, half = divmod(unit, halves)
        base = half * part_vocab
        sublane = lax.broadcasted_iota(jnp.int32, (8, 128), 0)
        for part in range(piece_rows // 128):
            own = pl.ds(piece * piece_rows + part * 128, 128)

            def load(group):
                values = logits_ref[slot, pl.ds(group * 8, 8), pl.ds(part * 128, 128)]
                if base + (group + 1) * 8 > last_valid:
                    left = vocab_cols - tile * tile_vocab - base - group * 8
                    values = jnp.where(sublane < left, values, lowest)
                return values

            groups = part_vocab // 8
            ways = 4
            tops = [load(group) for group in range(ways)]
            for group in range(ways, groups):
                tops[group % ways] = jnp.maximum(tops[group % ways], load(group))
            before = peak_ref[:, own]
            peak = functools.reduce(jnp.maximum, tops, before)
            change = before - peak
            factor = jnp.exp(change)
            total = total_ref[:, own]
            spread = factor * (spread_ref[:, own] + change * total)
            total = total * factor
            picked = picked_ref[:, own]
            offset = offset_ref[:, own]
            totals = [total] + [jnp.zeros_like(total)] * (ways - 1)
            spreads = [spread] + [jnp.zeros_like(total)] * (ways - 1)
            for group in range(groups):
                values = load(group)
                shifted = values - peak
                exponent = jnp.exp(shifted)
                totals[group % ways] = totals[group % ways] + exponent
                spreads[group % ways] = spreads[group % ways] + exponent * shifted
                picked = jnp.where(offset == tile * tile_vocab + base + group * 8, values, picked)
            peak_ref[:, own] = peak
            total_ref[:, own] = (totals[0] + totals[1]) + (totals[2] + totals[3])
            spread_ref[:, own] = (spreads[0] + spreads[1]) + (spreads[2] + spreads[3])
            picked_ref[:, own] = picked

    for unit in range(units):
        piece, half = divmod(unit, halves)
        logits_ref[unit % 2] = jnp.dot(
            weight_ref[pl.ds(half * part_vocab, part_vocab), :],
            rows_ref[:depth, pl.ds(piece * piece_rows, piece_rows)],
            preferred_element_type=f32,
        )
        if unit == 0:
            absorb(units - 1, step - 1)
        else:
            absorb(unit - 1, step)

    @pl.when(step == steps - 1)
    def _():
        absorb(units - 1, step)
        peak = peak_ref[...]
        total = total_ref[...]
        top = jnp.max(peak, axis=0, keepdims=True)
        change = peak - top
        factor = jnp.exp(change)
        out_ref[0:1, :] = top
        out_ref[1:2, :] = jnp.sum(total * factor, axis=0, keepdims=True)
        out_ref[2:3, :] = jnp.sum(factor * (spread_ref[...] + change * total), axis=0, keepdims=True)
        out_ref[3:4, :] = jnp.sum(picked_ref[...], axis=0, keepdims=True)


def block_stats(blocks, weight_rows):
    count = len(blocks)
    rows = count * live_cap
    vocab_cols, depth = weight_rows.shape
    steps = -(-vocab_cols // tile_vocab)
    return pl.pallas_call(
        functools.partial(stats_kernel, count, vocab_cols, steps),
        grid=(steps,),
        out_shape=(jax.ShapeDtypeStruct((4, rows), f32), jax.ShapeDtypeStruct((1, rows), f32)),
        in_specs=[pl.BlockSpec(memory_space=pl.ANY)] * count
        + [pl.BlockSpec((tile_vocab, depth), lambda step: (step, 0))],
        out_specs=(
            pl.BlockSpec((4, rows), lambda step: (0, 0)),
            pl.BlockSpec((1, rows), lambda step: (0, 0)),
        ),
        scratch_shapes=[
            pltpu.VMEM((depth + extra, rows), jnp.bfloat16),
            pltpu.VMEM((2, part_vocab, piece_rows), f32),
            pltpu.VMEM((8, rows), f32),
            pltpu.VMEM((8, rows), f32),
            pltpu.VMEM((8, rows), f32),
            pltpu.VMEM((8, rows), f32),
            pltpu.VMEM((8, rows), jnp.int32),
            pltpu.SemaphoreType.DMA((count,)),
        ],
        compiler_params=pltpu.CompilerParams(
            vmem_limit_bytes=vmem_bytes, dimension_semantics=("arbitrary",)
        ),
        cost_estimate=pl.CostEstimate(
            flops=2 * rows * depth * vocab_cols,
            bytes_accessed=2 * depth * vocab_cols,
            transcendentals=rows * vocab_cols,
        ),
        name="row_stats",
    )(*blocks, weight_rows)


def combine_kernel(order, *refs):
    peers = refs[: len(order)]
    meta_ref, out_ref = refs[len(order) :]
    for place in range(len(order[0])):
        own = pl.ds(place * live_cap, live_cap)
        parts = [peer[:, pl.ds(order[j][place] * live_cap, live_cap)] for j, peer in enumerate(peers)]
        top = functools.reduce(jnp.maximum, [part[0:1] for part in parts])
        total = jnp.zeros_like(top)
        spread = jnp.zeros_like(top)
        picked = jnp.zeros_like(top)
        for part in parts:
            change = part[0:1] - top
            factor = jnp.exp(change)
            total = total + part[1:2] * factor
            spread = spread + factor * (part[2:3] + change * part[1:2])
            picked = picked + part[3:4]
        log_total = jnp.log(total)
        out_ref[0:1, own] = picked - top - log_total
        out_ref[1:2, own] = log_total - spread / total
        out_ref[2:3, own] = meta_ref[:, own]
        out_ref[3:8, own] = jnp.zeros((5, live_cap), f32)


def combine(peers, order, meta):
    rows = meta.shape[1]
    return pl.pallas_call(
        functools.partial(combine_kernel, order),
        out_shape=jax.ShapeDtypeStruct((8, rows), f32),
        in_specs=[pl.BlockSpec(memory_space=pltpu.VMEM)] * (len(peers) + 1),
        out_specs=pl.BlockSpec(memory_space=pltpu.VMEM),
        compiler_params=pltpu.CompilerParams(vmem_limit_bytes=vmem_bytes),
        name="combine_stats",
    )(*peers, meta)


def pick_kernel(vocab_count, req_count, paired, seq_len, slot_ref, *refs):
    groups = refs[:req_count]
    logprob_ref, entropy_ref = refs[req_count:]
    seq_count = slot_ref.shape[0]
    req = lax.axis_index("req")
    vocab = lax.axis_index("vocab")
    lane = lax.broadcasted_iota(jnp.int32, (8, 128), 1)
    sublane = lax.broadcasted_iota(jnp.int32, (8, 128), 0)
    for request in range(seq_count):
        slot = slot_ref[request]
        owner = slot // seq_count
        within = slot - owner * seq_count
        owner_req = owner // vocab_count
        place = owner - owner_req * vocab_count
        if paired:
            place = place ^ vocab
        behind = lax.rem(req - owner_req + req_count, req_count)
        columns = pl.ds(pl.multiple_of(place * live_cap, live_cap), live_cap)
        block = groups[0][:, columns]
        for j in range(1, req_count):
            block = jnp.where(behind == j, groups[j][:, columns], block)
        meta = jnp.where(sublane == 2, block, 0.0)
        start = jnp.sum(jnp.where(lane == within, meta, 0.0), keepdims=True).astype(jnp.int32)
        length = jnp.sum(jnp.where(lane == seq_count + within, meta, 0.0), keepdims=True).astype(jnp.int32)
        index = jnp.minimum(start + lane, live_cap - 1)
        found = jnp.take_along_axis(block, index, axis=1, mode="promise_in_bounds")
        found = jnp.where(lane < length, found, 0.0)
        logprob_ref[request : request + 1, :] = found[0:1, :seq_len]
        entropy_ref[request : request + 1, :] = found[1:2, :seq_len]


def pick(slot_of, groups, vocab_count, paired, seq_len):
    shape = jax.ShapeDtypeStruct((slot_of.shape[0], seq_len), f32)
    return pl.pallas_call(
        functools.partial(pick_kernel, vocab_count, len(groups), paired, seq_len),
        out_shape=(shape, shape),
        in_specs=[pl.BlockSpec(memory_space=pltpu.SMEM)]
        + [pl.BlockSpec(memory_space=pltpu.VMEM)] * len(groups),
        out_specs=(pl.BlockSpec(memory_space=pltpu.VMEM), pl.BlockSpec(memory_space=pltpu.VMEM)),
        compiler_params=pltpu.CompilerParams(vmem_limit_bytes=vmem_bytes),
        name="pick_requests",
    )(slot_of, *groups)


def swap(array, mask, count):
    return lax.ppermute(array, "vocab", [(i, i ^ mask) for i in range(count)])


def local(vocab_count, req_count, hidden_states, norm_gain, head_weight, targets, lengths, slot_of):
    seq_len = hidden_states.shape[0] // lengths.shape[0]
    own = prepare(hidden_states, norm_gain, targets, lengths)
    weight_rows = head_weight.T
    paired = vocab_count == 8
    if paired:
        x_same = swap(own, 2, vocab_count)
        y_same = swap(own, 4, vocab_count)
        core = swap(own, 1, vocab_count)
        first = block_stats((own, core), weight_rows)
        x_other = swap(x_same, 1, vocab_count)
        y_other = swap(y_same, 1, vocab_count)
        half = own.shape[0] // 32 * 16
        diagonal = jnp.concatenate(
            (swap(x_same[:half], 4, vocab_count), swap(y_same[half:], 2, vocab_count)), axis=0
        )
        second = block_stats((x_same, x_other, y_same, y_other), weight_rows)
        diagonal_other = swap(diagonal, 1, vocab_count)
        third = block_stats((diagonal, diagonal_other), weight_rows)
        calls = (first, second, third)
        order = [[k ^ j for k in range(vocab_count)] for j in range(vocab_count)]
    else:
        gathered = lax.all_gather(own, "vocab", axis=0)
        calls = [
            block_stats([gathered[k] for k in range(at, min(at + 4, vocab_count))], weight_rows)
            for at in range(0, vocab_count, 4)
        ]
        order = [list(range(vocab_count))] * vocab_count
    stats = jnp.concatenate([call[0] for call in calls], axis=1)
    meta = jnp.concatenate([call[1] for call in calls], axis=1)
    if paired:
        peers = [stats] + [swap(stats, j, vocab_count) for j in range(1, vocab_count)]
    else:
        everyone = lax.all_gather(stats, "vocab", axis=0)
        peers = [everyone[j] for j in range(vocab_count)]
    result = combine(peers, order, meta)
    groups = [result] + [
        lax.ppermute(result, "req", [(i, (i + j) % req_count) for i in range(req_count)])
        for j in range(1, req_count)
    ]
    return pick(slot_of, groups, vocab_count, paired, seq_len)


def solution(mesh):
    in_specs = (
        P(("req", "vocab"), None),
        P(),
        P(None, "vocab"),
        P(("req", "vocab")),
        P(("req", "vocab")),
        P(("req", "vocab")),
    )
    out_specs = (P(("req", "vocab"), None), P(("req", "vocab"), None))
    body = functools.partial(local, mesh.shape["vocab"], mesh.shape["req"])
    return jax.shard_map(body, mesh=mesh, in_specs=in_specs, out_specs=out_specs, check_vma=False)
```

```python
import functools

import jax
import jax.numpy as jnp
from jax import lax
from jax.experimental import pallas as pl
from jax.experimental.pallas import tpu as pltpu
from jax.sharding import PartitionSpec as P

eps_norm = 1e-05
live_cap = 128
extra = 16
column_unit = 4000
lowest = -1e30
ahead = 3
places = (0, 1, 2, 4, 3, 5, 6, 7)
vmem_bytes = 10 * 1024 * 1024
f32 = jnp.float32


def prepare_kernel(
    lengths_in, hidden_in, gain_in, targets_in, out_ref, lengths_ref, hidden_ref, gain_ref, targets_ref, sems
):
    pairs = (
        (hidden_in, hidden_ref),
        (lengths_in, lengths_ref),
        (targets_in, targets_ref),
        (gain_in, gain_ref),
    )
    copies = [pltpu.make_async_copy(a, b, sems.at[i]) for i, (a, b) in enumerate(pairs)]
    for copy in copies:
        copy.start()
    for copy in copies:
        copy.wait()
    rows, depth = hidden_ref.shape
    seq_count = lengths_ref.shape[0]
    seq_len = rows // seq_count
    values = hidden_ref[...].astype(f32)
    inverse_rms = lax.rsqrt(jnp.mean(values * values, axis=1, keepdims=True) + eps_norm)
    normed = (values * inverse_rms * gain_ref[...]).astype(jnp.bfloat16)
    row = lax.broadcasted_iota(jnp.int32, (1, rows), 1)
    sublane = lax.broadcasted_iota(jnp.int32, (extra, live_cap), 0)
    lane = lax.broadcasted_iota(jnp.int32, (extra, live_cap), 1)
    place = jnp.full((1, rows), -1, jnp.int32)
    meta = jnp.zeros((extra, live_cap), jnp.int32)
    start = jnp.int32(0)
    for request in range(seq_count):
        length = lengths_ref[request]
        first = request * seq_len
        place = jnp.where((row >= first) & (row < first + length), row - first + start, place)
        meta = jnp.where(lane == request, start, meta)
        meta = jnp.where(lane == seq_count + request, length, meta)
        start = start + length
    chosen = lax.broadcasted_iota(jnp.int32, (live_cap, rows), 0) == place
    selector = chosen.astype(f32).astype(jnp.bfloat16)
    kept = jnp.dot(selector, normed, preferred_element_type=f32)
    for first in range(0, depth, 128):
        out_ref[first : first + 128, :] = kept[:, first : first + 128].T.astype(jnp.bfloat16)
    target = jnp.sum(jnp.where(chosen, targets_ref[...], 0), axis=1, keepdims=True)
    target = jnp.broadcast_to(target.astype(f32), (live_cap, 128)).T[:extra].astype(jnp.int32)
    meta = jnp.where(sublane == 0, target >> 8, meta)
    meta = jnp.where(sublane == 1, target & 255, meta)
    out_ref[depth:, :] = meta.astype(f32).astype(jnp.bfloat16)


def prepare(hidden_states, norm_gain, targets, lengths):
    rows, depth = hidden_states.shape
    return pl.pallas_call(
        prepare_kernel,
        out_shape=jax.ShapeDtypeStruct((depth + extra, live_cap), jnp.bfloat16),
        in_specs=[pl.BlockSpec(memory_space=pltpu.HBM)] * 4,
        out_specs=pl.BlockSpec(memory_space=pltpu.VMEM),
        scratch_shapes=[
            pltpu.SMEM(lengths.shape, jnp.int32),
            pltpu.VMEM((rows, depth), jnp.bfloat16),
            pltpu.VMEM((1, depth), f32),
            pltpu.VMEM((1, rows), jnp.int32),
            pltpu.SemaphoreType.DMA((4,)),
        ],
        compiler_params=pltpu.CompilerParams(vmem_limit_bytes=6 * vmem_bytes),
        name="prepare_rows",
    )(lengths, hidden_states, norm_gain.reshape(1, depth), targets.reshape(1, rows))


def stats_kernel(block_count, vocab_cols, steps, halves, piece_rows, mode, *refs):
    blocks = refs[:block_count]
    weight_ref = refs[block_count]
    if mode == "load":
        weight_in, weight_ref, sems = weight_ref, refs[block_count + 3], refs[-1]
        refs = refs[: block_count + 3] + refs[block_count + 4 : -1]
    out_ref, meta_ref = refs[-10:-8]
    rows_ref, even_ref, odd_ref, peak_ref, total_ref, spread_ref, picked_ref, offset_ref = refs[-8:]
    logits_refs = (even_ref, odd_ref)
    depth = weight_ref.shape[1]
    rows = block_count * live_cap
    part_vocab = even_ref.shape[0]
    tile_vocab = part_vocab * halves
    units = rows // piece_rows * halves
    vocab_start = lax.axis_index("vocab") * vocab_cols
    last_valid = vocab_cols - (steps - 1) * tile_vocab

    def arrival(index):
        own = pl.ds(pl.multiple_of(index * part_vocab, 16), part_vocab)
        return pltpu.make_async_copy(weight_in.at[own], weight_ref.at[own], sems.at[index])

    def begin():
        if mode == "load":
            for index in range(ahead):
                arrival(index).start(priority=index % 2)
        for place, block in enumerate(blocks):
            rows_ref[:, pl.ds(place * live_cap, live_cap)] = block[...]
        peak_ref[...] = jnp.full(peak_ref.shape, lowest, f32)
        total_ref[...] = jnp.zeros(total_ref.shape, f32)
        spread_ref[...] = jnp.zeros(spread_ref.shape, f32)
        picked_ref[...] = jnp.zeros(picked_ref.shape, f32)
        if steps > 1:
            logits_refs[(units - 1) % 2][...] = jnp.full(even_ref.shape, lowest, f32)
        digits = rows_ref[depth:, :].astype(f32)
        target = (digits[0:1] * 256.0 + digits[1:2]).astype(jnp.int32) - vocab_start
        target = jnp.where((target >= 0) & (target < vocab_cols), target, 2 * steps * tile_vocab)
        offset_ref[...] = target - lax.broadcasted_iota(jnp.int32, (8, rows), 0)
        meta_ref[...] = digits[2:3]

    def absorb(unit, tile):
        logits_ref = logits_refs[unit % 2]
        piece, half = divmod(unit, halves)
        base = half * part_vocab
        sublane = lax.broadcasted_iota(jnp.int32, (8, 128), 0)
        for part in range(piece_rows // 128):
            own = pl.ds(piece * piece_rows + part * 128, 128)

            def load(group):
                values = logits_ref[pl.ds(group * 8, 8), pl.ds(part * 128, 128)]
                if base + (group + 1) * 8 > last_valid:
                    left = vocab_cols - tile * tile_vocab - base - group * 8
                    values = jnp.where(sublane < left, values, lowest)
                return values

            groups = part_vocab // 8
            ways = 4
            tops = [load(group) for group in range(ways)]
            for group in range(ways, groups):
                tops[group % ways] = jnp.maximum(tops[group % ways], load(group))
            before = peak_ref[:, own]
            peak = functools.reduce(jnp.maximum, tops, before)
            change = before - peak
            factor = jnp.exp(change)
            total = total_ref[:, own]
            spread = factor * (spread_ref[:, own] + change * total)
            total = total * factor
            picked = picked_ref[:, own]
            offset = offset_ref[:, own]
            totals = [total] + [jnp.zeros_like(total)] * (ways - 1)
            spreads = [spread] + [jnp.zeros_like(total)] * (ways - 1)
            for group in range(groups):
                values = load(group)
                shifted = values - peak
                exponent = jnp.exp(shifted)
                totals[group % ways] = totals[group % ways] + exponent
                spreads[group % ways] = spreads[group % ways] + exponent * shifted
                picked = jnp.where(offset == tile * tile_vocab + base + group * 8, values, picked)
            peak_ref[:, own] = peak
            total_ref[:, own] = (totals[0] + totals[1]) + (totals[2] + totals[3])
            spread_ref[:, own] = (spreads[0] + spreads[1]) + (spreads[2] + spreads[3])
            picked_ref[:, own] = picked

    def advance(step, first):
        for unit in range(units):
            piece, half = divmod(unit, halves)
            at = first + half * part_vocab
            if steps > 1:
                at = pl.multiple_of(at, 16)
            if mode == "load" and piece == 0:
                index = step * halves + half
                arrival(index).wait()

                @pl.when(index + ahead < steps * halves)
                def _():
                    arrival(index + ahead).start(priority=(half + ahead) % 2)

            logits_refs[unit % 2][...] = jnp.dot(
                weight_ref[pl.ds(at, part_vocab), :],
                rows_ref[:depth, pl.ds(piece * piece_rows, piece_rows)],
                preferred_element_type=f32,
            )
            if unit == 0 and steps > 1:
                absorb(units - 1, step - 1)
            if unit > 0:
                absorb(unit - 1, step)

    def finish():
        absorb(units - 1, steps - 1)
        peak = peak_ref[...]
        total = total_ref[...]
        top = jnp.max(peak, axis=0, keepdims=True)
        change = peak - top
        factor = jnp.exp(change)
        out_ref[0:1, :] = top
        out_ref[1:2, :] = jnp.sum(total * factor, axis=0, keepdims=True)
        out_ref[2:3, :] = jnp.sum(factor * (spread_ref[...] + change * total), axis=0, keepdims=True)
        out_ref[3:4, :] = jnp.sum(picked_ref[...], axis=0, keepdims=True)

    if mode != "stream" and steps == 1:
        begin()
        advance(0, 0)
        finish()
    elif mode != "stream":
        begin()

        @pl.loop(0, steps)
        def _(step):
            advance(step, step * tile_vocab)

        finish()
    else:
        step = pl.program_id(0)
        pl.when(step == 0)(begin)
        advance(step, 0)
        pl.when(step == steps - 1)(finish)


def block_stats(blocks, weight_rows, mode, part_vocab=400, halves=2, piece_rows=256):
    count = len(blocks)
    rows = count * live_cap
    vocab_cols, depth = weight_rows.shape
    tile_vocab = part_vocab * halves
    steps = -(-vocab_cols // tile_vocab)
    whole = pl.BlockSpec(memory_space=pltpu.VMEM)
    shapes = (jax.ShapeDtypeStruct((4, rows), f32), jax.ShapeDtypeStruct((1, rows), f32))
    scratch = [
        pltpu.VMEM((depth + extra, rows), jnp.bfloat16),
        pltpu.VMEM((part_vocab, piece_rows), f32),
        pltpu.VMEM((part_vocab, piece_rows), f32),
        pltpu.VMEM((8, rows), f32),
        pltpu.VMEM((8, rows), f32),
        pltpu.VMEM((8, rows), f32),
        pltpu.VMEM((8, rows), f32),
        pltpu.VMEM((8, rows), jnp.int32),
    ]
    limit = vmem_bytes
    if mode == "stream":
        limit = 4 * vmem_bytes
        specs = dict(
            grid=(steps,),
            in_specs=[pl.BlockSpec((depth + extra, live_cap), lambda step: (0, 0))] * count
            + [pl.BlockSpec((tile_vocab, depth), lambda step: (step, 0))],
            out_specs=(
                pl.BlockSpec((4, rows), lambda step: (0, 0)),
                pl.BlockSpec((1, rows), lambda step: (0, 0)),
            ),
        )
    elif mode == "load":
        limit = 3 * vmem_bytes
        specs = dict(
            in_specs=[whole] * count + [pl.BlockSpec(memory_space=pltpu.HBM)], out_specs=(whole, whole, whole)
        )
        shapes = shapes + (jax.ShapeDtypeStruct(weight_rows.shape, weight_rows.dtype),)
        scratch = scratch + [pltpu.SemaphoreType.DMA((vocab_cols // part_vocab,))]
    else:
        specs = dict(in_specs=[whole] * (count + 1), out_specs=(whole, whole))
    return pl.pallas_call(
        functools.partial(stats_kernel, count, vocab_cols, steps, halves, piece_rows, mode),
        out_shape=shapes,
        scratch_shapes=scratch,
        compiler_params=pltpu.CompilerParams(vmem_limit_bytes=limit),
        cost_estimate=pl.CostEstimate(
            flops=2 * rows * depth * vocab_cols,
            bytes_accessed=2 * depth * (vocab_cols if mode == "load" else rows),
            transcendentals=rows * vocab_cols,
        ),
        name="row_stats",
        **specs,
    )(*blocks, weight_rows)


def merge(parts):
    top = functools.reduce(jnp.maximum, [part[0:1] for part in parts])
    total = jnp.zeros_like(top)
    spread = jnp.zeros_like(top)
    picked = jnp.zeros_like(top)
    for part in parts:
        change = part[0:1] - top
        factor = jnp.exp(change)
        total = total + part[1:2] * factor
        spread = spread + factor * (part[2:3] + change * part[1:2])
        picked = picked + part[3:4]
    return top, total, spread, picked


def merge_kernel(there_of, mine_ref, other_ref, out_ref):
    for place, there in enumerate(there_of):
        own = pl.ds(place * live_cap, live_cap)
        there = pl.ds(there * live_cap, live_cap)
        for row, value in enumerate(merge((mine_ref[:, own], other_ref[:, there]))):
            out_ref[row : row + 1, own] = value


def merge_pair(there_of, mine, other):
    return pl.pallas_call(
        functools.partial(merge_kernel, there_of),
        out_shape=jax.ShapeDtypeStruct(mine.shape, f32),
        in_specs=[pl.BlockSpec(memory_space=pltpu.VMEM)] * 2,
        out_specs=pl.BlockSpec(memory_space=pltpu.VMEM),
        compiler_params=pltpu.CompilerParams(vmem_limit_bytes=vmem_bytes),
        name="merge_stats",
    )(mine, other)


def result_kernel(order, *refs):
    peers = refs[: len(order)]
    meta_ref, out_ref = refs[len(order) :]
    for place in range(len(order[0])):
        own = pl.ds(place * live_cap, live_cap)
        top, total, spread, picked = merge(
            [peer[:, pl.ds(order[j][place] * live_cap, live_cap)] for j, peer in enumerate(peers)]
        )
        log_total = jnp.log(total)
        out_ref[0:1, own] = picked - top - log_total
        out_ref[1:2, own] = log_total - spread / total
        out_ref[2:3, own] = meta_ref[:, own]
        out_ref[3:4, own] = jnp.zeros((1, live_cap), f32)


def finish_rows(peers, order, meta):
    rows = meta.shape[1]
    return pl.pallas_call(
        functools.partial(result_kernel, order),
        out_shape=jax.ShapeDtypeStruct((4, rows), f32),
        in_specs=[pl.BlockSpec(memory_space=pltpu.VMEM)] * (len(peers) + 1),
        out_specs=pl.BlockSpec(memory_space=pltpu.VMEM),
        compiler_params=pltpu.CompilerParams(vmem_limit_bytes=vmem_bytes),
        name="finish_rows",
    )(*peers, meta)


def pick_kernel(vocab_count, paired, seq_len, slot_ref, near_ref, far_ref, logprob_ref, entropy_ref, *found_refs):
    seq_count = slot_ref.shape[0]
    req = lax.axis_index("req")
    vocab = lax.axis_index("vocab")
    half = near_ref.shape[0] // 4
    lane = lax.broadcasted_iota(jnp.int32, (seq_count, 128), 1)
    sublane = lax.broadcasted_iota(jnp.int32, (seq_count, 128), 0)
    within_all = jnp.zeros((seq_count, 128), jnp.int32)
    for request in range(seq_count):
        slot = slot_ref[request]
        owner = slot // seq_count
        owner_req = owner // vocab_count
        place = owner - owner_req * vocab_count
        if paired:
            block = place ^ vocab
            place = jnp.int32(0)
            for k in range(vocab_count):
                place = jnp.where(block == k, places[k], place)
        columns = pl.ds(pl.multiple_of(place * live_cap, live_cap), live_cap)
        apart = owner_req ^ req
        chosen = jnp.zeros((4, live_cap), f32)
        for j in range(half):
            chosen = jnp.where(apart == j, near_ref[4 * j : 4 * j + 4, columns], chosen)
            chosen = jnp.where(apart == j + half, far_ref[4 * j : 4 * j + 4, columns], chosen)
        for row, found_ref in enumerate(found_refs):
            found_ref[request : request + 1, :] = chosen[row : row + 1]
        within_all = jnp.where(sublane == request, slot - owner * seq_count, within_all)
    meta = found_refs[2][...]
    start = jnp.sum(jnp.where(lane == within_all, meta, 0.0), axis=1, keepdims=True).astype(jnp.int32)
    length = jnp.sum(jnp.where(lane == seq_count + within_all, meta, 0.0), axis=1, keepdims=True).astype(jnp.int32)
    index = jnp.minimum(start + lane, live_cap - 1)
    for found_ref, result_ref in zip(found_refs, (logprob_ref, entropy_ref)):
        found = jnp.take_along_axis(found_ref[...], index, axis=1, mode="promise_in_bounds")
        result_ref[...] = jnp.where(lane < length, found, 0.0)[:, :seq_len]


def pick(slot_of, near, far, vocab_count, paired, seq_len):
    seq_count = slot_of.shape[0]
    shape = jax.ShapeDtypeStruct((seq_count, seq_len), f32)
    whole = pl.BlockSpec(memory_space=pltpu.VMEM)
    return pl.pallas_call(
        functools.partial(pick_kernel, vocab_count, paired, seq_len),
        out_shape=(shape, shape),
        in_specs=[pl.BlockSpec(memory_space=pltpu.SMEM), whole, whole],
        out_specs=(whole, whole),
        scratch_shapes=[pltpu.VMEM((seq_count, live_cap), f32)] * 3,
        compiler_params=pltpu.CompilerParams(vmem_limit_bytes=vmem_bytes),
        name="pick_requests",
    )(slot_of, near, far)


def there_of(mask):
    blocks = sorted(range(len(places)), key=lambda k: places[k])
    return [places[k ^ mask] for k in blocks]


def swap(array, mask, count):
    return lax.ppermute(array, "vocab", [(i, i ^ mask) for i in range(count)])


def local(vocab_count, req_count, hidden_states, norm_gain, head_weight, targets, lengths, slot_of):
    seq_len = hidden_states.shape[0] // lengths.shape[0]
    own = prepare(hidden_states, norm_gain, targets, lengths)
    weight_rows = head_weight.T
    paired = vocab_count == 8 and head_weight.shape[1] % column_unit == 0
    if paired:
        x_same = swap(own, 2, vocab_count)
        y_same = swap(own, 4, vocab_count)
        core = swap(own, 1, vocab_count)
        *first, weight_rows = block_stats((own, core), weight_rows, "load")
        x_same, y_same, weight_rows = lax.optimization_barrier((x_same, y_same, weight_rows))
        half = own.shape[0] // 32 * 16
        diagonal_low = swap(x_same[:half], 4, vocab_count)
        diagonal_high = swap(y_same[half:], 2, vocab_count)
        x_other = swap(x_same, 1, vocab_count)
        y_other = swap(y_same, 1, vocab_count)
        second = block_stats((x_same, y_same), weight_rows, "resident", 800, 5)
        diagonal_low, diagonal_high, *second = lax.optimization_barrier((diagonal_low, diagonal_high, *second))
        diagonal = jnp.concatenate((diagonal_low, diagonal_high), axis=0)
        diagonal_other = swap(diagonal, 1, vocab_count)
        third = block_stats((x_other, y_other, diagonal, diagonal_other), weight_rows, "resident", 400, 2, 512)
        calls = (first, second, third)
    else:
        gathered = lax.all_gather(own, "vocab", axis=0)
        calls = [
            block_stats([gathered[k] for k in range(at, min(at + 4, vocab_count))], weight_rows, "stream")
            for at in range(0, vocab_count, 4)
        ]
    stats = jnp.concatenate([call[0] for call in calls], axis=1)
    meta = jnp.concatenate([call[1] for call in calls], axis=1)
    if paired:
        for mask in (1, 2):
            stats = merge_pair(there_of(mask), stats, swap(stats, mask, vocab_count))
        peers = (stats, swap(stats, 4, vocab_count))
        order = [there_of(0), there_of(4)]
    else:
        everyone = lax.all_gather(stats, "vocab", axis=0)
        peers = [everyone[j] for j in range(vocab_count)]
        order = [list(range(vocab_count))] * vocab_count
    near = finish_rows(peers, order, meta)
    mask = 1
    while True:
        far = lax.ppermute(near, "req", [(i, i ^ mask) for i in range(req_count)])
        mask = 2 * mask
        if mask == req_count:
            break
        near = jnp.concatenate((near, far), axis=0)
    return pick(slot_of, near, far, vocab_count, paired, seq_len)


def solution(mesh):
    in_specs = (
        P(("req", "vocab"), None),
        P(),
        P(None, "vocab"),
        P(("req", "vocab")),
        P(("req", "vocab")),
        P(("req", "vocab")),
    )
    out_specs = (P(("req", "vocab"), None), P(("req", "vocab"), None))
    body = functools.partial(local, mesh.shape["vocab"], mesh.shape["req"])
    return jax.shard_map(body, mesh=mesh, in_specs=in_specs, out_specs=out_specs, check_vma=False)
```

```python
import functools

import jax
import jax.numpy as jnp
from jax import lax
from jax.experimental import pallas as pl
from jax.experimental.pallas import tpu as pltpu
from jax.sharding import PartitionSpec as P

eps_norm = 1e-05
live_cap = 128
extra = 16
column_unit = 4000
lowest = -1e30
ahead = 3
places = (0, 1, 2, 4, 3, 5, 6, 7)
vmem_bytes = 10 * 1024 * 1024
f32 = jnp.float32


def prepare_kernel(
    lengths_in, hidden_in, gain_in, targets_in, out_ref, lengths_ref, hidden_ref, gain_ref, targets_ref, sems
):
    pairs = (
        (hidden_in, hidden_ref),
        (lengths_in, lengths_ref),
        (targets_in, targets_ref),
        (gain_in, gain_ref),
    )
    copies = [pltpu.make_async_copy(a, b, sems.at[i]) for i, (a, b) in enumerate(pairs)]
    for copy in copies:
        copy.start()
    for copy in copies:
        copy.wait()
    rows, depth = hidden_ref.shape
    seq_count = lengths_ref.shape[0]
    seq_len = rows // seq_count
    values = hidden_ref[...].astype(f32)
    inverse_rms = lax.rsqrt(jnp.mean(values * values, axis=1, keepdims=True) + eps_norm)
    normed = (values * inverse_rms * gain_ref[...]).astype(jnp.bfloat16)
    row = lax.broadcasted_iota(jnp.int32, (1, rows), 1)
    sublane = lax.broadcasted_iota(jnp.int32, (extra, live_cap), 0)
    lane = lax.broadcasted_iota(jnp.int32, (extra, live_cap), 1)
    place = jnp.full((1, rows), -1, jnp.int32)
    meta = jnp.zeros((extra, live_cap), jnp.int32)
    start = jnp.int32(0)
    for request in range(seq_count):
        length = lengths_ref[request]
        first = request * seq_len
        place = jnp.where((row >= first) & (row < first + length), row - first + start, place)
        meta = jnp.where(lane == request, start, meta)
        meta = jnp.where(lane == seq_count + request, length, meta)
        start = start + length
    chosen = lax.broadcasted_iota(jnp.int32, (live_cap, rows), 0) == place
    selector = chosen.astype(f32).astype(jnp.bfloat16)
    kept = jnp.dot(selector, normed, preferred_element_type=f32)
    for first in range(0, depth, 128):
        out_ref[first : first + 128, :] = kept[:, first : first + 128].T.astype(jnp.bfloat16)
    target = jnp.sum(jnp.where(chosen, targets_ref[...], 0), axis=1, keepdims=True)
    target = jnp.broadcast_to(target.astype(f32), (live_cap, 128)).T[:extra].astype(jnp.int32)
    meta = jnp.where(sublane == 0, target >> 8, meta)
    meta = jnp.where(sublane == 1, target & 255, meta)
    out_ref[depth:, :] = meta.astype(f32).astype(jnp.bfloat16)


def prepare(hidden_states, norm_gain, targets, lengths):
    rows, depth = hidden_states.shape
    return pl.pallas_call(
        prepare_kernel,
        out_shape=jax.ShapeDtypeStruct((depth + extra, live_cap), jnp.bfloat16),
        in_specs=[pl.BlockSpec(memory_space=pltpu.HBM)] * 4,
        out_specs=pl.BlockSpec(memory_space=pltpu.VMEM),
        scratch_shapes=[
            pltpu.SMEM(lengths.shape, jnp.int32),
            pltpu.VMEM((rows, depth), jnp.bfloat16),
            pltpu.VMEM((1, depth), f32),
            pltpu.VMEM((1, rows), jnp.int32),
            pltpu.SemaphoreType.DMA((4,)),
        ],
        compiler_params=pltpu.CompilerParams(vmem_limit_bytes=6 * vmem_bytes),
        name="prepare_rows",
    )(lengths, hidden_states, norm_gain.reshape(1, depth), targets.reshape(1, rows))


def stats_kernel(block_count, vocab_cols, steps, halves, piece_rows, mode, *refs):
    blocks = refs[:block_count]
    weight_ref = refs[block_count]
    if mode == "load":
        weight_in, weight_ref, sems = weight_ref, refs[block_count + 3], refs[-1]
        refs = refs[: block_count + 3] + refs[block_count + 4 : -1]
    out_ref, meta_ref = refs[-10:-8]
    rows_ref, even_ref, odd_ref, peak_ref, total_ref, spread_ref, picked_ref, offset_ref = refs[-8:]
    logits_refs = (even_ref, odd_ref)
    depth = weight_ref.shape[1]
    rows = block_count * live_cap
    part_vocab = even_ref.shape[0]
    tile_vocab = part_vocab * halves
    units = rows // piece_rows * halves
    vocab_start = lax.axis_index("vocab") * vocab_cols
    last_valid = vocab_cols - (steps - 1) * tile_vocab

    def arrival(index):
        own = pl.ds(pl.multiple_of(index * part_vocab, 16), part_vocab)
        return pltpu.make_async_copy(weight_in.at[own], weight_ref.at[own], sems.at[index])

    def begin():
        if mode == "load":
            for index in range(ahead):
                arrival(index).start()
        for place, block in enumerate(blocks):
            rows_ref[:, pl.ds(place * live_cap, live_cap)] = block[...]
        peak_ref[...] = jnp.full(peak_ref.shape, lowest, f32)
        total_ref[...] = jnp.zeros(total_ref.shape, f32)
        spread_ref[...] = jnp.zeros(spread_ref.shape, f32)
        picked_ref[...] = jnp.zeros(picked_ref.shape, f32)
        if steps > 1:
            logits_refs[(units - 1) % 2][...] = jnp.full(even_ref.shape, lowest, f32)
        digits = rows_ref[depth:, :].astype(f32)
        target = (digits[0:1] * 256.0 + digits[1:2]).astype(jnp.int32) - vocab_start
        target = jnp.where((target >= 0) & (target < vocab_cols), target, 2 * steps * tile_vocab)
        offset_ref[...] = target - lax.broadcasted_iota(jnp.int32, (8, rows), 0)
        meta_ref[...] = digits[2:3]

    def absorb(unit, tile):
        logits_ref = logits_refs[unit % 2]
        piece, half = divmod(unit, halves)
        base = half * part_vocab
        sublane = lax.broadcasted_iota(jnp.int32, (8, 128), 0)
        for part in range(piece_rows // 128):
            own = pl.ds(piece * piece_rows + part * 128, 128)

            def load(group):
                values = logits_ref[pl.ds(group * 8, 8), pl.ds(part * 128, 128)]
                if base + (group + 1) * 8 > last_valid:
                    left = vocab_cols - tile * tile_vocab - base - group * 8
                    values = jnp.where(sublane < left, values, lowest)
                return values

            groups = part_vocab // 8
            ways = 4
            tops = [load(group) for group in range(ways)]
            for group in range(ways, groups):
                tops[group % ways] = jnp.maximum(tops[group % ways], load(group))
            before = peak_ref[:, own]
            peak = functools.reduce(jnp.maximum, tops, before)
            change = before - peak
            factor = jnp.exp(change)
            total = total_ref[:, own]
            spread = factor * (spread_ref[:, own] + change * total)
            total = total * factor
            picked = picked_ref[:, own]
            offset = offset_ref[:, own]
            totals = [total] + [jnp.zeros_like(total)] * (ways - 1)
            spreads = [spread] + [jnp.zeros_like(total)] * (ways - 1)
            for group in range(groups):
                values = load(group)
                shifted = values - peak
                exponent = jnp.exp(shifted)
                totals[group % ways] = totals[group % ways] + exponent
                spreads[group % ways] = spreads[group % ways] + exponent * shifted
                picked = jnp.where(offset == tile * tile_vocab + base + group * 8, values, picked)
            peak_ref[:, own] = peak
            total_ref[:, own] = (totals[0] + totals[1]) + (totals[2] + totals[3])
            spread_ref[:, own] = (spreads[0] + spreads[1]) + (spreads[2] + spreads[3])
            picked_ref[:, own] = picked

    def advance(step, first):
        for unit in range(units):
            piece, half = divmod(unit, halves)
            at = first + half * part_vocab
            if steps > 1:
                at = pl.multiple_of(at, 16)
            if mode == "load" and piece == 0:
                index = step * halves + half
                arrival(index).wait()

                @pl.when(index + ahead < steps * halves)
                def _():
                    arrival(index + ahead).start()

            logits_refs[unit % 2][...] = jnp.dot(
                weight_ref[pl.ds(at, part_vocab), :],
                rows_ref[:depth, pl.ds(piece * piece_rows, piece_rows)],
                preferred_element_type=f32,
            )
            if unit == 0 and steps > 1:
                absorb(units - 1, step - 1)
            if unit > 0:
                absorb(unit - 1, step)

    def finish():
        absorb(units - 1, steps - 1)
        peak = peak_ref[...]
        total = total_ref[...]
        top = jnp.max(peak, axis=0, keepdims=True)
        change = peak - top
        factor = jnp.exp(change)
        out_ref[0:1, :] = top
        out_ref[1:2, :] = jnp.sum(total * factor, axis=0, keepdims=True)
        out_ref[2:3, :] = jnp.sum(factor * (spread_ref[...] + change * total), axis=0, keepdims=True)
        out_ref[3:4, :] = jnp.sum(picked_ref[...], axis=0, keepdims=True)

    if mode != "stream" and steps == 1:
        begin()
        advance(0, 0)
        finish()
    elif mode != "stream":
        begin()

        @pl.loop(0, steps)
        def _(step):
            advance(step, step * tile_vocab)

        finish()
    else:
        step = pl.program_id(0)
        pl.when(step == 0)(begin)
        advance(step, 0)
        pl.when(step == steps - 1)(finish)


def block_stats(blocks, weight_rows, mode, part_vocab=400, halves=2, piece_rows=256):
    count = len(blocks)
    rows = count * live_cap
    vocab_cols, depth = weight_rows.shape
    tile_vocab = part_vocab * halves
    steps = -(-vocab_cols // tile_vocab)
    whole = pl.BlockSpec(memory_space=pltpu.VMEM)
    shapes = (jax.ShapeDtypeStruct((4, rows), f32), jax.ShapeDtypeStruct((1, rows), f32))
    scratch = [
        pltpu.VMEM((depth + extra, rows), jnp.bfloat16),
        pltpu.VMEM((part_vocab, piece_rows), f32),
        pltpu.VMEM((part_vocab, piece_rows), f32),
        pltpu.VMEM((8, rows), f32),
        pltpu.VMEM((8, rows), f32),
        pltpu.VMEM((8, rows), f32),
        pltpu.VMEM((8, rows), f32),
        pltpu.VMEM((8, rows), jnp.int32),
    ]
    limit = vmem_bytes
    if mode == "stream":
        limit = 4 * vmem_bytes
        specs = dict(
            grid=(steps,),
            in_specs=[pl.BlockSpec((depth + extra, live_cap), lambda step: (0, 0))] * count
            + [pl.BlockSpec((tile_vocab, depth), lambda step: (step, 0))],
            out_specs=(
                pl.BlockSpec((4, rows), lambda step: (0, 0)),
                pl.BlockSpec((1, rows), lambda step: (0, 0)),
            ),
        )
    elif mode == "load":
        limit = 3 * vmem_bytes
        specs = dict(
            in_specs=[whole] * count + [pl.BlockSpec(memory_space=pltpu.HBM)], out_specs=(whole, whole, whole)
        )
        shapes = shapes + (jax.ShapeDtypeStruct(weight_rows.shape, weight_rows.dtype),)
        scratch = scratch + [pltpu.SemaphoreType.DMA((vocab_cols // part_vocab,))]
    else:
        specs = dict(in_specs=[whole] * (count + 1), out_specs=(whole, whole))
    return pl.pallas_call(
        functools.partial(stats_kernel, count, vocab_cols, steps, halves, piece_rows, mode),
        out_shape=shapes,
        scratch_shapes=scratch,
        compiler_params=pltpu.CompilerParams(vmem_limit_bytes=limit),
        cost_estimate=pl.CostEstimate(
            flops=2 * rows * depth * vocab_cols,
            bytes_accessed=2 * depth * (vocab_cols if mode == "load" else rows),
            transcendentals=rows * vocab_cols,
        ),
        name="row_stats",
        **specs,
    )(*blocks, weight_rows)


def merge(parts):
    top = functools.reduce(jnp.maximum, [part[0:1] for part in parts])
    total = jnp.zeros_like(top)
    spread = jnp.zeros_like(top)
    picked = jnp.zeros_like(top)
    for part in parts:
        change = part[0:1] - top
        factor = jnp.exp(change)
        total = total + part[1:2] * factor
        spread = spread + factor * (part[2:3] + change * part[1:2])
        picked = picked + part[3:4]
    return top, total, spread, picked


def merge_kernel(there_of, mine_ref, other_ref, out_ref):
    for place, there in enumerate(there_of):
        own = pl.ds(place * live_cap, live_cap)
        there = pl.ds(there * live_cap, live_cap)
        for row, value in enumerate(merge((mine_ref[:, own], other_ref[:, there]))):
            out_ref[row : row + 1, own] = value


def merge_pair(there_of, mine, other):
    return pl.pallas_call(
        functools.partial(merge_kernel, there_of),
        out_shape=jax.ShapeDtypeStruct(mine.shape, f32),
        in_specs=[pl.BlockSpec(memory_space=pltpu.VMEM)] * 2,
        out_specs=pl.BlockSpec(memory_space=pltpu.VMEM),
        compiler_params=pltpu.CompilerParams(vmem_limit_bytes=vmem_bytes),
        name="merge_stats",
    )(mine, other)


def result_kernel(order, *refs):
    peers = refs[: len(order)]
    meta_ref, out_ref = refs[len(order) :]
    for place in range(len(order[0])):
        own = pl.ds(place * live_cap, live_cap)
        top, total, spread, picked = merge(
            [peer[:, pl.ds(order[j][place] * live_cap, live_cap)] for j, peer in enumerate(peers)]
        )
        log_total = jnp.log(total)
        out_ref[0:1, own] = picked - top - log_total
        out_ref[1:2, own] = log_total - spread / total
        out_ref[2:3, own] = meta_ref[:, own]
        out_ref[3:4, own] = jnp.zeros((1, live_cap), f32)


def finish_rows(peers, order, meta):
    rows = meta.shape[1]
    return pl.pallas_call(
        functools.partial(result_kernel, order),
        out_shape=jax.ShapeDtypeStruct((4, rows), f32),
        in_specs=[pl.BlockSpec(memory_space=pltpu.VMEM)] * (len(peers) + 1),
        out_specs=pl.BlockSpec(memory_space=pltpu.VMEM),
        compiler_params=pltpu.CompilerParams(vmem_limit_bytes=vmem_bytes),
        name="finish_rows",
    )(*peers, meta)


def pick_kernel(vocab_count, paired, seq_len, slot_ref, near_ref, far_ref, logprob_ref, entropy_ref, *found_refs):
    seq_count = slot_ref.shape[0]
    req = lax.axis_index("req")
    vocab = lax.axis_index("vocab")
    half = near_ref.shape[0] // 4
    lane = lax.broadcasted_iota(jnp.int32, (seq_count, 128), 1)
    sublane = lax.broadcasted_iota(jnp.int32, (seq_count, 128), 0)
    within_all = jnp.zeros((seq_count, 128), jnp.int32)
    for request in range(seq_count):
        slot = slot_ref[request]
        owner = slot // seq_count
        owner_req = owner // vocab_count
        place = owner - owner_req * vocab_count
        if paired:
            block = place ^ vocab
            place = jnp.int32(0)
            for k in range(vocab_count):
                place = jnp.where(block == k, places[k], place)
        columns = pl.ds(pl.multiple_of(place * live_cap, live_cap), live_cap)
        apart = owner_req ^ req
        chosen = jnp.zeros((4, live_cap), f32)
        for j in range(half):
            chosen = jnp.where(apart == j, near_ref[4 * j : 4 * j + 4, columns], chosen)
            chosen = jnp.where(apart == j + half, far_ref[4 * j : 4 * j + 4, columns], chosen)
        for row, found_ref in enumerate(found_refs):
            found_ref[request : request + 1, :] = chosen[row : row + 1]
        within_all = jnp.where(sublane == request, slot - owner * seq_count, within_all)
    meta = found_refs[2][...]
    start = jnp.sum(jnp.where(lane == within_all, meta, 0.0), axis=1, keepdims=True).astype(jnp.int32)
    length = jnp.sum(jnp.where(lane == seq_count + within_all, meta, 0.0), axis=1, keepdims=True).astype(jnp.int32)
    index = jnp.minimum(start + lane, live_cap - 1)
    for found_ref, result_ref in zip(found_refs, (logprob_ref, entropy_ref)):
        found = jnp.take_along_axis(found_ref[...], index, axis=1, mode="promise_in_bounds")
        result_ref[...] = jnp.where(lane < length, found, 0.0)[:, :seq_len]


def pick(slot_of, near, far, vocab_count, paired, seq_len):
    seq_count = slot_of.shape[0]
    shape = jax.ShapeDtypeStruct((seq_count, seq_len), f32)
    whole = pl.BlockSpec(memory_space=pltpu.VMEM)
    return pl.pallas_call(
        functools.partial(pick_kernel, vocab_count, paired, seq_len),
        out_shape=(shape, shape),
        in_specs=[pl.BlockSpec(memory_space=pltpu.SMEM), whole, whole],
        out_specs=(whole, whole),
        scratch_shapes=[pltpu.VMEM((seq_count, live_cap), f32)] * 3,
        compiler_params=pltpu.CompilerParams(vmem_limit_bytes=vmem_bytes),
        name="pick_requests",
    )(slot_of, near, far)


def there_of(mask):
    blocks = sorted(range(len(places)), key=lambda k: places[k])
    return [places[k ^ mask] for k in blocks]


def swap(array, mask, count):
    return lax.ppermute(array, "vocab", [(i, i ^ mask) for i in range(count)])


def local(vocab_count, req_count, hidden_states, norm_gain, head_weight, targets, lengths, slot_of):
    seq_len = hidden_states.shape[0] // lengths.shape[0]
    own = prepare(hidden_states, norm_gain, targets, lengths)
    weight_rows = head_weight.T
    paired = vocab_count == 8 and head_weight.shape[1] % column_unit == 0
    if paired:
        x_same = swap(own, 2, vocab_count)
        y_same = swap(own, 4, vocab_count)
        core = swap(own, 1, vocab_count)
        *first, weight_rows = block_stats((own, core), weight_rows, "load")
        x_same, y_same, weight_rows = lax.optimization_barrier((x_same, y_same, weight_rows))
        half = own.shape[0] // 32 * 16
        diagonal_low = swap(x_same[:half], 4, vocab_count)
        diagonal_high = swap(y_same[half:], 2, vocab_count)
        x_other = swap(x_same, 1, vocab_count)
        y_other = swap(y_same, 1, vocab_count)
        second = block_stats((x_same, y_same), weight_rows, "resident", 800, 5)
        diagonal_low, diagonal_high, *second = lax.optimization_barrier((diagonal_low, diagonal_high, *second))
        diagonal = jnp.concatenate((diagonal_low, diagonal_high), axis=0)
        diagonal_other = swap(diagonal, 1, vocab_count)
        third = block_stats((x_other, y_other), weight_rows, "resident", 800, 5)
        fourth = block_stats((diagonal, diagonal_other), weight_rows, "resident", 800, 5)
        calls = (first, second, third, fourth)
    else:
        gathered = lax.all_gather(own, "vocab", axis=0)
        calls = [
            block_stats([gathered[k] for k in range(at, min(at + 4, vocab_count))], weight_rows, "stream")
            for at in range(0, vocab_count, 4)
        ]
    stats = jnp.concatenate([call[0] for call in calls], axis=1)
    meta = jnp.concatenate([call[1] for call in calls], axis=1)
    if paired:
        for mask in (1, 2):
            stats = merge_pair(there_of(mask), stats, swap(stats, mask, vocab_count))
        peers = (stats, swap(stats, 4, vocab_count))
        order = [there_of(0), there_of(4)]
    else:
        everyone = lax.all_gather(stats, "vocab", axis=0)
        peers = [everyone[j] for j in range(vocab_count)]
        order = [list(range(vocab_count))] * vocab_count
    near = finish_rows(peers, order, meta)
    mask = 1
    while True:
        far = lax.ppermute(near, "req", [(i, i ^ mask) for i in range(req_count)])
        mask = 2 * mask
        if mask == req_count:
            break
        near = jnp.concatenate((near, far), axis=0)
    return pick(slot_of, near, far, vocab_count, paired, seq_len)


def solution(mesh):
    in_specs = (
        P(("req", "vocab"), None),
        P(),
        P(None, "vocab"),
        P(("req", "vocab")),
        P(("req", "vocab")),
        P(("req", "vocab")),
    )
    out_specs = (P(("req", "vocab"), None), P(("req", "vocab"), None))
    body = functools.partial(local, mesh.shape["vocab"], mesh.shape["req"])
    return jax.shard_map(body, mesh=mesh, in_specs=in_specs, out_specs=out_specs, check_vma=False)
```

```python
import functools

import jax
import jax.numpy as jnp
from jax import lax
from jax.experimental import pallas as pl
from jax.experimental.pallas import tpu as pltpu
from jax.sharding import PartitionSpec as P

eps_norm = 1e-05
live_cap = 128
extra = 16
column_unit = 4000
lowest = -1e30
ahead = 3
places = (0, 1, 2, 4, 3, 5, 6, 7)
vmem_bytes = 10 * 1024 * 1024
f32 = jnp.float32


def prepare_kernel(
    lengths_in, hidden_in, gain_in, targets_in, out_ref, lengths_ref, hidden_ref, gain_ref, targets_ref, sems
):
    pairs = (
        (hidden_in, hidden_ref),
        (lengths_in, lengths_ref),
        (targets_in, targets_ref),
        (gain_in, gain_ref),
    )
    copies = [pltpu.make_async_copy(a, b, sems.at[i]) for i, (a, b) in enumerate(pairs)]
    for copy in copies:
        copy.start()
    for copy in copies:
        copy.wait()
    rows, depth = hidden_ref.shape
    seq_count = lengths_ref.shape[0]
    seq_len = rows // seq_count
    values = hidden_ref[...].astype(f32)
    inverse_rms = lax.rsqrt(jnp.mean(values * values, axis=1, keepdims=True) + eps_norm)
    normed = (values * inverse_rms * gain_ref[...]).astype(jnp.bfloat16)
    row = lax.broadcasted_iota(jnp.int32, (1, rows), 1)
    sublane = lax.broadcasted_iota(jnp.int32, (extra, live_cap), 0)
    lane = lax.broadcasted_iota(jnp.int32, (extra, live_cap), 1)
    place = jnp.full((1, rows), -1, jnp.int32)
    meta = jnp.zeros((extra, live_cap), jnp.int32)
    start = jnp.int32(0)
    for request in range(seq_count):
        length = lengths_ref[request]
        first = request * seq_len
        place = jnp.where((row >= first) & (row < first + length), row - first + start, place)
        meta = jnp.where(lane == request, start, meta)
        meta = jnp.where(lane == seq_count + request, length, meta)
        start = start + length
    chosen = lax.broadcasted_iota(jnp.int32, (live_cap, rows), 0) == place
    selector = chosen.astype(f32).astype(jnp.bfloat16)
    kept = jnp.dot(selector, normed, preferred_element_type=f32)
    for first in range(0, depth, 128):
        out_ref[first : first + 128, :] = kept[:, first : first + 128].T.astype(jnp.bfloat16)
    target = jnp.sum(jnp.where(chosen, targets_ref[...], 0), axis=1, keepdims=True)
    target = jnp.broadcast_to(target.astype(f32), (live_cap, 128)).T[:extra].astype(jnp.int32)
    meta = jnp.where(sublane == 0, target >> 8, meta)
    meta = jnp.where(sublane == 1, target & 255, meta)
    out_ref[depth:, :] = meta.astype(f32).astype(jnp.bfloat16)


def prepare(hidden_states, norm_gain, targets, lengths):
    rows, depth = hidden_states.shape
    return pl.pallas_call(
        prepare_kernel,
        out_shape=jax.ShapeDtypeStruct((depth + extra, live_cap), jnp.bfloat16),
        in_specs=[pl.BlockSpec(memory_space=pltpu.HBM)] * 4,
        out_specs=pl.BlockSpec(memory_space=pltpu.VMEM),
        scratch_shapes=[
            pltpu.SMEM(lengths.shape, jnp.int32),
            pltpu.VMEM((rows, depth), jnp.bfloat16),
            pltpu.VMEM((1, depth), f32),
            pltpu.VMEM((1, rows), jnp.int32),
            pltpu.SemaphoreType.DMA((4,)),
        ],
        compiler_params=pltpu.CompilerParams(vmem_limit_bytes=6 * vmem_bytes),
        name="prepare_rows",
    )(lengths, hidden_states, norm_gain.reshape(1, depth), targets.reshape(1, rows))


def stats_kernel(block_count, vocab_cols, steps, halves, piece_rows, mode, *refs):
    blocks = refs[:block_count]
    weight_ref = refs[block_count]
    if mode == "load":
        weight_in, weight_ref, sems = weight_ref, refs[block_count + 3], refs[-1]
        refs = refs[: block_count + 3] + refs[block_count + 4 : -1]
    out_ref, meta_ref = refs[-10:-8]
    rows_ref, even_ref, odd_ref, peak_ref, total_ref, spread_ref, picked_ref, offset_ref = refs[-8:]
    logits_refs = (even_ref, odd_ref)
    depth = weight_ref.shape[1]
    rows = block_count * live_cap
    part_vocab = even_ref.shape[0]
    tile_vocab = part_vocab * halves
    units = rows // piece_rows * halves
    vocab_start = lax.axis_index("vocab") * vocab_cols
    last_valid = vocab_cols - (steps - 1) * tile_vocab

    def arrival(index):
        own = pl.ds(pl.multiple_of(index * part_vocab, 16), part_vocab)
        return pltpu.make_async_copy(weight_in.at[own], weight_ref.at[own], sems.at[index])

    def begin():
        if mode == "load":
            for index in range(ahead):
                arrival(index).start()
        for place, block in enumerate(blocks):
            rows_ref[:, pl.ds(place * live_cap, live_cap)] = block[...]
        peak_ref[...] = jnp.full(peak_ref.shape, lowest, f32)
        total_ref[...] = jnp.zeros(total_ref.shape, f32)
        spread_ref[...] = jnp.zeros(spread_ref.shape, f32)
        picked_ref[...] = jnp.zeros(picked_ref.shape, f32)
        if steps > 1:
            logits_refs[(units - 1) % 2][...] = jnp.full(even_ref.shape, lowest, f32)
        digits = rows_ref[depth:, :].astype(f32)
        target = (digits[0:1] * 256.0 + digits[1:2]).astype(jnp.int32) - vocab_start
        target = jnp.where((target >= 0) & (target < vocab_cols), target, 2 * steps * tile_vocab)
        offset_ref[...] = target - lax.broadcasted_iota(jnp.int32, (8, rows), 0)
        meta_ref[...] = digits[2:3]

    def absorb(unit, tile):
        logits_ref = logits_refs[unit % 2]
        piece, half = divmod(unit, halves)
        base = half * part_vocab
        sublane = lax.broadcasted_iota(jnp.int32, (8, 128), 0)
        for part in range(piece_rows // 128):
            own = pl.ds(piece * piece_rows + part * 128, 128)

            def load(group):
                values = logits_ref[pl.ds(group * 8, 8), pl.ds(part * 128, 128)]
                if base + (group + 1) * 8 > last_valid:
                    left = vocab_cols - tile * tile_vocab - base - group * 8
                    values = jnp.where(sublane < left, values, lowest)
                return values

            groups = part_vocab // 8
            ways = 4
            tops = [load(group) for group in range(ways)]
            for group in range(ways, groups):
                tops[group % ways] = jnp.maximum(tops[group % ways], load(group))
            before = peak_ref[:, own]
            peak = functools.reduce(jnp.maximum, tops, before)
            change = before - peak
            factor = jnp.exp(change)
            total = total_ref[:, own]
            spread = factor * (spread_ref[:, own] + change * total)
            total = total * factor
            picked = picked_ref[:, own]
            offset = offset_ref[:, own]
            totals = [total] + [jnp.zeros_like(total)] * (ways - 1)
            spreads = [spread] + [jnp.zeros_like(total)] * (ways - 1)
            for group in range(groups):
                values = load(group)
                shifted = values - peak
                exponent = jnp.exp(shifted)
                totals[group % ways] = totals[group % ways] + exponent
                spreads[group % ways] = spreads[group % ways] + exponent * shifted
                picked = jnp.where(offset == tile * tile_vocab + base + group * 8, values, picked)
            peak_ref[:, own] = peak
            total_ref[:, own] = (totals[0] + totals[1]) + (totals[2] + totals[3])
            spread_ref[:, own] = (spreads[0] + spreads[1]) + (spreads[2] + spreads[3])
            picked_ref[:, own] = picked

    def advance(step, first):
        for unit in range(units):
            piece, half = divmod(unit, halves)
            at = first + half * part_vocab
            if steps > 1:
                at = pl.multiple_of(at, 16)
            if mode == "load" and piece == 0:
                index = step * halves + half
                arrival(index).wait()

                @pl.when(index + ahead < steps * halves)
                def _():
                    arrival(index + ahead).start()

            logits_refs[unit % 2][...] = jnp.dot(
                weight_ref[pl.ds(at, part_vocab), :],
                rows_ref[:depth, pl.ds(piece * piece_rows, piece_rows)],
                preferred_element_type=f32,
            )
            if unit == 0 and steps > 1:
                absorb(units - 1, step - 1)
            if unit > 0:
                absorb(unit - 1, step)

    def finish():
        absorb(units - 1, steps - 1)
        peak = peak_ref[...]
        total = total_ref[...]
        top = jnp.max(peak, axis=0, keepdims=True)
        change = peak - top
        factor = jnp.exp(change)
        out_ref[0:1, :] = top
        out_ref[1:2, :] = jnp.sum(total * factor, axis=0, keepdims=True)
        out_ref[2:3, :] = jnp.sum(factor * (spread_ref[...] + change * total), axis=0, keepdims=True)
        out_ref[3:4, :] = jnp.sum(picked_ref[...], axis=0, keepdims=True)

    if mode != "stream" and steps == 1:
        begin()
        advance(0, 0)
        finish()
    elif mode != "stream":
        begin()

        @pl.loop(0, steps)
        def _(step):
            advance(step, step * tile_vocab)

        finish()
    else:
        step = pl.program_id(0)
        pl.when(step == 0)(begin)
        advance(step, 0)
        pl.when(step == steps - 1)(finish)


def block_stats(blocks, weight_rows, mode, part_vocab=400, halves=2, piece_rows=256):
    count = len(blocks)
    rows = count * live_cap
    vocab_cols, depth = weight_rows.shape
    tile_vocab = part_vocab * halves
    steps = -(-vocab_cols // tile_vocab)
    whole = pl.BlockSpec(memory_space=pltpu.VMEM)
    shapes = (jax.ShapeDtypeStruct((4, rows), f32), jax.ShapeDtypeStruct((1, rows), f32))
    scratch = [
        pltpu.VMEM((depth + extra, rows), jnp.bfloat16),
        pltpu.VMEM((part_vocab, piece_rows), f32),
        pltpu.VMEM((part_vocab, piece_rows), f32),
        pltpu.VMEM((8, rows), f32),
        pltpu.VMEM((8, rows), f32),
        pltpu.VMEM((8, rows), f32),
        pltpu.VMEM((8, rows), f32),
        pltpu.VMEM((8, rows), jnp.int32),
    ]
    limit = vmem_bytes
    if mode == "stream":
        limit = 4 * vmem_bytes
        specs = dict(
            grid=(steps,),
            in_specs=[pl.BlockSpec((depth + extra, live_cap), lambda step: (0, 0))] * count
            + [pl.BlockSpec((tile_vocab, depth), lambda step: (step, 0))],
            out_specs=(
                pl.BlockSpec((4, rows), lambda step: (0, 0)),
                pl.BlockSpec((1, rows), lambda step: (0, 0)),
            ),
        )
    elif mode == "load":
        limit = 3 * vmem_bytes
        specs = dict(
            in_specs=[whole] * count + [pl.BlockSpec(memory_space=pltpu.HBM)], out_specs=(whole, whole, whole)
        )
        shapes = shapes + (jax.ShapeDtypeStruct(weight_rows.shape, weight_rows.dtype),)
        scratch = scratch + [pltpu.SemaphoreType.DMA((vocab_cols // part_vocab,))]
    else:
        specs = dict(in_specs=[whole] * (count + 1), out_specs=(whole, whole))
    return pl.pallas_call(
        functools.partial(stats_kernel, count, vocab_cols, steps, halves, piece_rows, mode),
        out_shape=shapes,
        scratch_shapes=scratch,
        compiler_params=pltpu.CompilerParams(vmem_limit_bytes=limit),
        cost_estimate=pl.CostEstimate(
            flops=2 * rows * depth * vocab_cols,
            bytes_accessed=2 * depth * (vocab_cols if mode == "load" else rows),
            transcendentals=rows * vocab_cols,
        ),
        name="row_stats",
        **specs,
    )(*blocks, weight_rows)


def merge(parts):
    top = functools.reduce(jnp.maximum, [part[0:1] for part in parts])
    total = jnp.zeros_like(top)
    spread = jnp.zeros_like(top)
    picked = jnp.zeros_like(top)
    for part in parts:
        change = part[0:1] - top
        factor = jnp.exp(change)
        total = total + part[1:2] * factor
        spread = spread + factor * (part[2:3] + change * part[1:2])
        picked = picked + part[3:4]
    return top, total, spread, picked


def merge_kernel(there_of, mine_ref, other_ref, out_ref):
    for place, there in enumerate(there_of):
        own = pl.ds(place * live_cap, live_cap)
        there = pl.ds(there * live_cap, live_cap)
        for row, value in enumerate(merge((mine_ref[:, own], other_ref[:, there]))):
            out_ref[row : row + 1, own] = value


def merge_pair(there_of, mine, other):
    return pl.pallas_call(
        functools.partial(merge_kernel, there_of),
        out_shape=jax.ShapeDtypeStruct(mine.shape, f32),
        in_specs=[pl.BlockSpec(memory_space=pltpu.VMEM)] * 2,
        out_specs=pl.BlockSpec(memory_space=pltpu.VMEM),
        compiler_params=pltpu.CompilerParams(vmem_limit_bytes=vmem_bytes),
        name="merge_stats",
    )(mine, other)


def result_kernel(order, *refs):
    peers = refs[: len(order)]
    meta_ref, out_ref = refs[len(order) :]
    for place in range(len(order[0])):
        own = pl.ds(place * live_cap, live_cap)
        top, total, spread, picked = merge(
            [peer[:, pl.ds(order[j][place] * live_cap, live_cap)] for j, peer in enumerate(peers)]
        )
        log_total = jnp.log(total)
        out_ref[0:1, own] = picked - top - log_total
        out_ref[1:2, own] = log_total - spread / total
        out_ref[2:3, own] = meta_ref[:, own]
        out_ref[3:4, own] = jnp.zeros((1, live_cap), f32)


def finish_rows(peers, order, meta):
    rows = meta.shape[1]
    return pl.pallas_call(
        functools.partial(result_kernel, order),
        out_shape=jax.ShapeDtypeStruct((4, rows), f32),
        in_specs=[pl.BlockSpec(memory_space=pltpu.VMEM)] * (len(peers) + 1),
        out_specs=pl.BlockSpec(memory_space=pltpu.VMEM),
        compiler_params=pltpu.CompilerParams(vmem_limit_bytes=vmem_bytes),
        name="finish_rows",
    )(*peers, meta)


def pick_kernel(vocab_count, paired, seq_len, slot_ref, near_ref, far_ref, logprob_ref, entropy_ref, *found_refs):
    seq_count = slot_ref.shape[0]
    req = lax.axis_index("req")
    vocab = lax.axis_index("vocab")
    half = near_ref.shape[0] // 4
    lane = lax.broadcasted_iota(jnp.int32, (seq_count, 128), 1)
    sublane = lax.broadcasted_iota(jnp.int32, (seq_count, 128), 0)
    within_all = jnp.zeros((seq_count, 128), jnp.int32)
    for request in range(seq_count):
        slot = slot_ref[request]
        owner = slot // seq_count
        owner_req = owner // vocab_count
        place = owner - owner_req * vocab_count
        if paired:
            block = place ^ vocab
            place = jnp.int32(0)
            for k in range(vocab_count):
                place = jnp.where(block == k, places[k], place)
        columns = pl.ds(pl.multiple_of(place * live_cap, live_cap), live_cap)
        apart = owner_req ^ req
        chosen = jnp.zeros((4, live_cap), f32)
        for j in range(half):
            chosen = jnp.where(apart == j, near_ref[4 * j : 4 * j + 4, columns], chosen)
            chosen = jnp.where(apart == j + half, far_ref[4 * j : 4 * j + 4, columns], chosen)
        for row, found_ref in enumerate(found_refs):
            found_ref[request : request + 1, :] = chosen[row : row + 1]
        within_all = jnp.where(sublane == request, slot - owner * seq_count, within_all)
    meta = found_refs[2][...]
    start = jnp.sum(jnp.where(lane == within_all, meta, 0.0), axis=1, keepdims=True).astype(jnp.int32)
    length = jnp.sum(jnp.where(lane == seq_count + within_all, meta, 0.0), axis=1, keepdims=True).astype(jnp.int32)
    index = jnp.minimum(start + lane, live_cap - 1)
    for found_ref, result_ref in zip(found_refs, (logprob_ref, entropy_ref)):
        found = jnp.take_along_axis(found_ref[...], index, axis=1, mode="promise_in_bounds")
        result_ref[...] = jnp.where(lane < length, found, 0.0)[:, :seq_len]


def pick(slot_of, near, far, vocab_count, paired, seq_len):
    seq_count = slot_of.shape[0]
    shape = jax.ShapeDtypeStruct((seq_count, seq_len), f32)
    whole = pl.BlockSpec(memory_space=pltpu.VMEM)
    return pl.pallas_call(
        functools.partial(pick_kernel, vocab_count, paired, seq_len),
        out_shape=(shape, shape),
        in_specs=[pl.BlockSpec(memory_space=pltpu.SMEM), whole, whole],
        out_specs=(whole, whole),
        scratch_shapes=[pltpu.VMEM((seq_count, live_cap), f32)] * 3,
        compiler_params=pltpu.CompilerParams(vmem_limit_bytes=vmem_bytes),
        name="pick_requests",
    )(slot_of, near, far)


def there_of(mask):
    blocks = sorted(range(len(places)), key=lambda k: places[k])
    return [places[k ^ mask] for k in blocks]


def swap(array, mask, count):
    return lax.ppermute(array, "vocab", [(i, i ^ mask) for i in range(count)])


def local(vocab_count, req_count, hidden_states, norm_gain, head_weight, targets, lengths, slot_of):
    seq_len = hidden_states.shape[0] // lengths.shape[0]
    own = prepare(hidden_states, norm_gain, targets, lengths)
    weight_rows = head_weight.T
    paired = vocab_count == 8 and head_weight.shape[1] % column_unit == 0
    if paired:
        x_same = swap(own, 2, vocab_count)
        y_same = swap(own, 4, vocab_count)
        core = swap(own, 1, vocab_count)
        *first, weight_rows = block_stats((own, core), weight_rows, "load", 800, 5)
        x_same, y_same, weight_rows = lax.optimization_barrier((x_same, y_same, weight_rows))
        half = own.shape[0] // 32 * 16
        diagonal_low = swap(x_same[:half], 4, vocab_count)
        diagonal_high = swap(y_same[half:], 2, vocab_count)
        x_other = swap(x_same, 1, vocab_count)
        y_other = swap(y_same, 1, vocab_count)
        second = block_stats((x_same, y_same), weight_rows, "resident", 800, 5)
        diagonal_low, diagonal_high, *second = lax.optimization_barrier((diagonal_low, diagonal_high, *second))
        diagonal = jnp.concatenate((diagonal_low, diagonal_high), axis=0)
        diagonal_other = swap(diagonal, 1, vocab_count)
        third = block_stats((x_other, y_other), weight_rows, "resident", 800, 5)
        fourth = block_stats((diagonal, diagonal_other), weight_rows, "resident", 800, 5)
        calls = (first, second, third, fourth)
    else:
        gathered = lax.all_gather(own, "vocab", axis=0)
        calls = [
            block_stats([gathered[k] for k in range(at, min(at + 4, vocab_count))], weight_rows, "stream")
            for at in range(0, vocab_count, 4)
        ]
    stats = jnp.concatenate([call[0] for call in calls], axis=1)
    meta = jnp.concatenate([call[1] for call in calls], axis=1)
    if paired:
        for mask in (1, 2):
            stats = merge_pair(there_of(mask), stats, swap(stats, mask, vocab_count))
        peers = (stats, swap(stats, 4, vocab_count))
        order = [there_of(0), there_of(4)]
    else:
        everyone = lax.all_gather(stats, "vocab", axis=0)
        peers = [everyone[j] for j in range(vocab_count)]
        order = [list(range(vocab_count))] * vocab_count
    near = finish_rows(peers, order, meta)
    mask = 1
    while True:
        far = lax.ppermute(near, "req", [(i, i ^ mask) for i in range(req_count)])
        mask = 2 * mask
        if mask == req_count:
            break
        near = jnp.concatenate((near, far), axis=0)
    return pick(slot_of, near, far, vocab_count, paired, seq_len)


def solution(mesh):
    in_specs = (
        P(("req", "vocab"), None),
        P(),
        P(None, "vocab"),
        P(("req", "vocab")),
        P(("req", "vocab")),
        P(("req", "vocab")),
    )
    out_specs = (P(("req", "vocab"), None), P(("req", "vocab"), None))
    body = functools.partial(local, mesh.shape["vocab"], mesh.shape["req"])
    return jax.shard_map(body, mesh=mesh, in_specs=in_specs, out_specs=out_specs, check_vma=False)
```
